32 devices in a mesh: section: 16 (over z, y, core), tensor: 2 (over x).
Axes of the slice: x: 2, y: 2, z: 4, core: 2. Of those that a mesh axis runs over, the one named last changes fastest.
Arguments:
- memory: bfloat16 [2, 12288, 4096], P(None, 'section', 'tensor'), may hold values from -4 to 4
- queries: bfloat16 [4096, 4096], P(('section', 'tensor')), may hold values from -6.5 to 6.5
- out_grad: bfloat16 [4096, 4096], P(('section', 'tensor')), may hold values from -6 to 6
- enc_lengths: int32 [16, 8], replicated, may hold values from 1 to 128, 768 in all within a row
- dec_lengths: int32 [16, 8], replicated, may hold values from 1 to 64, 256 in all within a row
- readers: int32 [16, 8], replicated, may hold values from 0 to 15, as said below
Outputs:
- attended: bfloat16 [4096, 4096], P(('section', 'tensor'))
- query_grad: bfloat16 [4096, 4096], P(('section', 'tensor'))
- memory_grad: bfloat16 [2, 12288, 4096], P(None, 'section', 'tensor')
The draws below stay inside these ranges and needn't reach their ends.
Inputs may be any that keep to these rules, and one draw needn't show every extreme that they name: `readers`: the reader of example j of encoder device s is (s + k * 2 + 1) modulo 16 for some k < 8; each encoder device names each of its 8 such devices exactly 1 times, so every decoder device is named exactly 8 times.
All inputs are finite; a program needn't handle non-finite values.
Results may differ from the reference program's by a relative error of at most 0.011.
Values may be sent and summed in bfloat16 or wider, within the bound.
A program may use at most 64 MiB of HBM per device.

```python
import math
import jax
import jax.numpy as jnp
import numpy as np
from jax import lax

HEADS = 32
HD = 128
EX_DEV = 8
ENC_MAX = 128
DEC_MAX = 64
PARTNERS = 8
ENC_DEV = 768
DEC_DEV = 256
ENC_TOKENS = 12288
DEC_TOKENS = 4096
N_SECTION = 16


def draw_memory(key, part):
    row_total = ENC_DEV * N_SECTION
    feature_width = HEADS * HD
    key_base = jax.random.fold_in(key, 0)
    baseline = jax.random.normal(key_base, (2, row_total, feature_width), jnp.float32)
    return jnp.clip(baseline, -4.0, 4.0).astype(jnp.bfloat16)


def draw_queries(key, part):
    row_total = DEC_DEV * N_SECTION
    feature_width = HEADS * HD
    key_base = jax.random.fold_in(key, 0)
    baseline = jax.random.normal(key_base, (row_total, feature_width), jnp.float32)
    return jnp.clip(baseline, -4.0, 4.0).astype(jnp.bfloat16)


def draw_readers(key, part):
    spacing = N_SECTION // PARTNERS
    order_keys = jax.random.split(key, N_SECTION)
    slot_order = jax.vmap(lambda single: jax.random.permutation(single, EX_DEV))(order_keys).astype(jnp.int32)
    partner_index = slot_order % PARTNERS
    holders = jnp.arange(N_SECTION, dtype=jnp.int32)[:, None]
    return ((holders + partner_index * spacing + 1) % N_SECTION).astype(jnp.int32)


def level_of(own_key, extent, cuts, low, largest):
    loudness, own = 1.0, jax.random.fold_in(own_key, 6)
    for dim, shards_of in cuts:
        heights = jnp.exp(jax.random.uniform(jax.random.fold_in(own, dim), (shards_of,), jnp.float32, low / len(cuts), largest / len(cuts)))
        loudness = loudness * jnp.repeat(heights, extent[dim] // shards_of).reshape([-1 if axis == dim else 1 for axis in range(len(extent))])
    return loudness


def length_profile(count, total, limit, skew):
    portions = [(1 << 20) // math.isqrt(grade ** skew) + 1 for grade in range(2, count + 1)]
    rest, given = total - limit - (count - 1), [1] * (count - 1)
    while rest > 0:
        movable = [i for i in range(count - 1) if given[i] < limit]
        pool, left = sum([portions[i] for i in movable]), rest
        for i in movable:
            more = min(limit - given[i], max(1, left * portions[i] // pool), rest)
            given[i] = given[i] + more
            rest = rest - more
    return np.array([limit] + given)


def uneven(own_key, count, total, limit, skew):
    if count == 2:
        one = jax.random.randint(own_key, (), max(1, total - limit), min(limit, total - 1) + 1)
        return jnp.stack([one, total - one])
    sizes = jnp.asarray(length_profile(count, total, limit, skew), jnp.int32)
    twos = (count - 1) // 2
    donor, receiver = sizes[1:1 + 2 * twos:2], sizes[2:2 + 2 * twos:2]
    margin = jnp.minimum(donor - 1, limit - receiver)
    shifted = jax.random.randint(jax.random.fold_in(own_key, 1), (twos,), 0, 1 << 20) % (margin + 1)
    sizes = sizes.at[1:1 + 2 * twos:2].set(donor - shifted).at[2:2 + 2 * twos:2].set(receiver + shifted)
    return sizes[jax.random.permutation(jax.random.fold_in(own_key, 2), count)]


def gaussian(stream_key, shape, spread, most, pieces=(), kind=jnp.bfloat16):
    drawn = spread * jax.random.normal(stream_key, shape, jnp.float32)
    if pieces:
        drawn = drawn * level_of(stream_key, shape, pieces, -0.22, 0.18)
    return jnp.clip(drawn, -most, most).astype(kind)


def setup_inputs(seed: int = 0) -> dict:
    streams_of = jax.random.split(jax.random.key(seed), 7)
    memory = draw_memory(jax.random.fold_in(streams_of[6], 71), 0)
    queries = draw_queries(jax.random.fold_in(streams_of[6], 71), 0)
    out_grad = gaussian(streams_of[2], (DEC_TOKENS, HEADS * HD), 1.0, 6.0, ((0, 32),))
    enc_lengths = jax.vmap(lambda own: uneven(own, EX_DEV, ENC_DEV, ENC_MAX, 2))(jax.random.split(streams_of[3], N_SECTION)).reshape((N_SECTION, EX_DEV)).astype(jnp.int32)
    dec_lengths = jax.vmap(lambda own: uneven(own, EX_DEV, DEC_DEV, DEC_MAX, 1))(jax.random.split(streams_of[4], N_SECTION)).reshape((N_SECTION, EX_DEV)).astype(jnp.int32)
    readers = draw_readers(jax.random.fold_in(streams_of[6], 71), 0)
    return dict(memory=memory, queries=queries, out_grad=out_grad, enc_lengths=enc_lengths, dec_lengths=dec_lengths, readers=readers)


def reference(memory, queries, out_grad, enc_lengths, dec_lengths, readers):
    feature_width = HEADS * HD
    scaling = HD ** -0.5
    flattened = readers.reshape(-1).astype(jnp.int32)
    everyone = jnp.arange(flattened.shape[0], dtype=jnp.int32)
    enc_bounds = jnp.cumsum(enc_lengths, axis=1).astype(jnp.int32)
    device_base = jnp.arange(N_SECTION, dtype=jnp.int32)[:, None] * ENC_DEV
    enc_start = (enc_bounds - enc_lengths + device_base).reshape(-1).astype(jnp.int32)
    enc_sizes = enc_lengths.reshape(-1).astype(jnp.int32)
    key_offsets = jnp.arange(ENC_MAX, dtype=jnp.int32)
    dec_offsets = jnp.arange(DEC_MAX, dtype=jnp.int32)
    labels = jnp.arange(EX_DEV, dtype=jnp.int32)
    positions = jnp.arange(DEC_DEV, dtype=jnp.int32)

    def per_reader(carry, reader):
        key_acc, value_acc = carry
        is_mine = (flattened == reader).astype(jnp.int32)
        ordinal = (jnp.cumsum(is_mine) - is_mine).astype(jnp.int32)
        matches = (is_mine[None, :] == 1) & (ordinal[None, :] == labels[:, None])
        example_ids = jnp.sum(jnp.where(matches, everyone[None, :], 0), axis=1).astype(jnp.int32)
        begins = enc_start[example_ids]
        sizes = enc_sizes[example_ids]
        key_valid = key_offsets[None, :] < sizes[:, None]
        key_rows = jnp.where(key_valid, begins[:, None] + key_offsets[None, :], 0).astype(jnp.int32)
        dec_row = lax.dynamic_index_in_dim(dec_lengths, reader, 0, keepdims=False).astype(jnp.int32)
        dec_bounds = jnp.cumsum(dec_row).astype(jnp.int32)
        dec_begin = (dec_bounds - dec_row).astype(jnp.int32)
        dec_valid = dec_offsets[None, :] < dec_row[:, None]
        dec_rows = jnp.where(dec_valid, reader * DEC_DEV + dec_begin[:, None] + dec_offsets[None, :], 0).astype(jnp.int32)
        block_shape = (EX_DEV, DEC_MAX, HEADS, HD)
        query_block = jnp.where(dec_valid[:, :, None], queries[dec_rows], 0).astype(jnp.float32).reshape(block_shape)
        grad_block = jnp.where(dec_valid[:, :, None], out_grad[dec_rows], 0).astype(jnp.float32).reshape(block_shape)
        key_block = memory[0][key_rows].astype(jnp.float32).reshape(EX_DEV, ENC_MAX, HEADS, HD)
        value_block = memory[1][key_rows].astype(jnp.float32).reshape(EX_DEV, ENC_MAX, HEADS, HD)
        scores = jnp.einsum("eqhd,ekhd->ehqk", query_block, key_block) * scaling
        scores = jnp.where(key_valid[:, None, None, :], scores, -jnp.inf)
        highest = jnp.max(scores, axis=3, keepdims=True)
        weights = jnp.exp(scores - highest)
        probabilities = weights / jnp.sum(weights, axis=3, keepdims=True)
        probs_low = lax.optimization_barrier(probabilities.astype(jnp.bfloat16)).astype(jnp.float32)
        attended = jnp.einsum("ehqk,ekhd->eqhd", probs_low, value_block).astype(jnp.bfloat16).reshape(EX_DEV * DEC_MAX, feature_width)
        dprobs = jnp.einsum("eqhd,ekhd->ehqk", grad_block, value_block)
        row_delta = jnp.sum(probabilities * dprobs, axis=3, keepdims=True)
        dscores = lax.optimization_barrier((probabilities * (dprobs - row_delta)).astype(jnp.bfloat16)).astype(jnp.float32)
        query_grad = (jnp.einsum("ehqk,ekhd->eqhd", dscores, key_block) * scaling).astype(jnp.bfloat16).reshape(EX_DEV * DEC_MAX, feature_width)
        key_terms = (jnp.einsum("ehqk,eqhd->ekhd", dscores, query_block) * scaling).astype(jnp.bfloat16).reshape(-1, feature_width)
        value_terms = jnp.einsum("ehqk,eqhd->ekhd", probs_low, grad_block).astype(jnp.bfloat16).reshape(-1, feature_width)
        flat_valid = key_valid.reshape(-1, 1)
        flat_rows = key_rows.reshape(-1)
        key_acc = key_acc.at[flat_rows].add(jnp.where(flat_valid, key_terms, jnp.zeros((), key_terms.dtype)))
        value_acc = value_acc.at[flat_rows].add(jnp.where(flat_valid, value_terms, jnp.zeros((), value_terms.dtype)))
        member = jnp.sum((positions[:, None] >= dec_bounds[None, :]).astype(jnp.int32), axis=1).astype(jnp.int32)
        token_index = (member * DEC_MAX + positions - dec_begin[member]).astype(jnp.int32)
        return (key_acc, value_acc), (attended[token_index], query_grad[token_index])

    zero_acc = jnp.zeros((ENC_TOKENS, feature_width), jnp.bfloat16)
    (key_acc, value_acc), (attended, query_grad) = lax.scan(per_reader, (zero_acc, zero_acc), jnp.arange(N_SECTION, dtype=jnp.int32))
    memory_grad = jnp.stack([key_acc, value_acc])
    return attended.reshape(-1, feature_width), query_grad.reshape(-1, feature_width), memory_grad
```

```python
import functools

import jax
import jax.numpy as jnp
from jax import lax
from jax.experimental import pallas as pl
from jax.experimental.pallas import tpu as pltpu
from jax.sharding import PartitionSpec as P

HD = 128
ENC_MAX = 128
DEC_MAX = 64
PARTNERS = 8
CHUNKS = 4
BF16 = jnp.bfloat16
F32 = jnp.float32
MESH = pl.DeviceIdType.MESH


def matmul(a, b, dims):
    return lax.dot_general(a, b, (dims, ((), ())), preferred_element_type=F32)


NN = ((1,), (0,))
NT = ((1,), (1,))
TN = ((0,), (0,))


def kernel(
    sections,
    tensors,
    mem_hbm,
    q_hbm,
    g_hbm,
    enc_len,
    dec_len,
    readers,
    att_hbm,
    qg_hbm,
    mg_hbm,
    mem_v,
    dec_v,
    fsend,
    frecv,
    osend,
    oret,
    fin_v,
    kv_x,
    d_x,
    pack_m,
    unpack_m,
    enc_m,
    grad_m,
    meta,
    a_send,
    a_recv,
    a_local,
    f_send,
    f_recv,
    o_send,
    o_recv,
    g_send,
    g_recv,
    g_local,
    m_in,
    m_out,
):
    me = lax.axis_index("section")
    mine = lax.axis_index("tensor")
    rows = q_hbm.shape[0]
    enc_count = mem_v.shape[1]
    dec_count = dec_v.shape[2]
    width = mem_v.shape[2]
    piece = width // CHUNKS
    spacing = sections // PARTNERS
    scaling = HD ** (-0.5)

    def holder_of(slot):
        return lax.rem(me + 2 * sections - slot * spacing - 1, sections)

    def reader_of(slot):
        return lax.rem(me + slot * spacing + 1, sections)

    def peer_of(step):
        return lax.rem(mine + step, tensors)

    mem_copy = pltpu.make_async_copy(mem_hbm, mem_v, m_in)
    mem_copy.start()

    barrier = pltpu.get_barrier_semaphore()
    for step in range(1, tensors):
        pl.semaphore_signal(
            barrier, inc=1, device_id={"tensor": peer_of(step)}, device_id_type=MESH
        )
    for slot in range(PARTNERS):
        pl.semaphore_signal(
            barrier, inc=1, device_id={"section": holder_of(slot)}, device_id_type=MESH
        )
        pl.semaphore_signal(
            barrier, inc=1, device_id={"section": reader_of(slot)}, device_id_type=MESH
        )
    pl.semaphore_wait(barrier, tensors - 1 + 2 * PARTNERS)

    own_rows = pl.ds(pl.multiple_of(mine * rows, rows), rows)

    def first_copy(c, a, step):
        peer = peer_of(step)
        source = (q_hbm, g_hbm)[a]
        columns = pl.ds(pl.multiple_of(peer * width + c * piece, piece), piece)
        if step == 0:
            return pltpu.make_async_copy(
                source.at[:, columns], dec_v.at[c, a, own_rows], a_local.at[c, a]
            )
        return pltpu.make_async_remote_copy(
            src_ref=source.at[:, columns],
            dst_ref=dec_v.at[c, a, own_rows],
            send_sem=a_send.at[c, a, step - 1],
            recv_sem=a_recv.at[c, a, step - 1],
            device_id={"tensor": peer},
            device_id_type=MESH,
        )

    for c in range(CHUNKS):
        for a in range(2):
            for step in list(range(1, tensors)) + [0]:
                first_copy(c, a, step).start()

    start = jnp.int32(0)
    for i in range(PARTNERS):
        length = dec_len[me, i]
        meta[0, i] = start
        meta[1, i] = length
        start = start + length
    for slot in range(PARTNERS):
        reader = reader_of(slot)
        start, begin, size = jnp.int32(0), jnp.int32(0), jnp.int32(0)
        for j in range(PARTNERS):
            length = enc_len[me, j]
            match = readers[me, j] == reader
            begin = jnp.where(match, start, begin)
            size = jnp.where(match, length, size)
            start = start + length
        meta[2, slot] = begin
        meta[3, slot] = size

    def one_hot(hits):
        return jnp.where(hits, 1.0, 0.0).astype(BF16)

    def iota(shape, dim):
        return lax.broadcasted_iota(jnp.int32, shape, dim)

    half = PARTNERS // 2
    for i in range(PARTNERS):
        shape = (DEC_MAX, dec_count)
        within = iota(shape, 0)
        hits = (iota(shape, 1) - within == meta[0, i]) & (within < meta[1, i])
        pack_m[i // half, (i % half) * DEC_MAX : (i % half + 1) * DEC_MAX, :] = one_hot(hits)

    def forward_copy(c, slot):
        holder = holder_of(slot)
        return pltpu.make_async_remote_copy(
            src_ref=fsend.at[c, :, lax.div(holder, spacing)],
            dst_ref=frecv.at[c, :, slot],
            send_sem=f_send.at[c, slot],
            recv_sem=f_recv.at[c, slot],
            device_id={"section": holder},
            device_id_type=MESH,
        )

    def back_copy(c, slot):
        return pltpu.make_async_remote_copy(
            src_ref=osend.at[c, :, slot],
            dst_ref=oret.at[c, :, lax.div(me, spacing)],
            send_sem=o_send.at[c, slot],
            recv_sem=o_recv.at[c, lax.div(me, spacing)],
            device_id={"section": reader_of(slot)},
            device_id_type=MESH,
        )

    def back_arrival(c, i):
        return pltpu.make_async_remote_copy(
            src_ref=osend.at[c, :, i],
            dst_ref=oret.at[c, :, i],
            send_sem=o_send.at[c, i],
            recv_sem=o_recv.at[c, i],
            device_id={"section": reader_of(i)},
            device_id_type=MESH,
        )

    def last_copy(c, a, step):
        peer = peer_of(step)
        target = (att_hbm, qg_hbm)[a]
        source = fin_v.at[c, a, pl.ds(pl.multiple_of(peer * rows, rows), rows)]
        columns = pl.ds(pl.multiple_of(mine * width + c * piece, piece), piece)
        if step == 0:
            return pltpu.make_async_copy(source, target.at[:, columns], g_local.at[c, a])
        return pltpu.make_async_remote_copy(
            src_ref=source,
            dst_ref=target.at[:, columns],
            send_sem=g_send.at[c, a, step - 1],
            recv_sem=g_recv.at[c, a, step - 1],
            device_id={"tensor": peer},
            device_id_type=MESH,
        )

    def grad_copy(c):
        columns = pl.ds(c * piece, piece)
        return pltpu.make_async_copy(
            mem_v.at[:, :, columns], mg_hbm.at[:, :, columns], m_out.at[c]
        )

    def pack(c):
        for a in range(2):
            first_copy(c, a, 0).wait()
            for step in range(1, tensors):
                first_copy(c, a, step).wait_recv()
        for a in range(2):
            for g in range(2):
                block = matmul(pack_m[g], dec_v[c, a], NN).astype(BF16)
                fsend[c, a, g * half : (g + 1) * half] = block.reshape(half, DEC_MAX, piece)

        @pl.loop(0, PARTNERS)
        def _(slot):
            forward_copy(c, slot).start()

    def expand(c):
        @pl.loop(0, PARTNERS // 2)
        def _(g):
            for a in range(2):
                block = matmul(enc_m[g], mem_v[a, :, c * piece : (c + 1) * piece], NN)
                kv_x[c, a, pl.ds(g * 2, 2)] = block.astype(BF16).reshape(2, ENC_MAX, piece)

    def attend(c):
        @pl.loop(0, PARTNERS)
        def _(slot):
            forward_copy(c, slot).wait_recv()
            valid = iota((DEC_MAX, ENC_MAX), 1) < meta[3, slot]
            for h in range(piece // HD):
                at = slice(h * HD, (h + 1) * HD)
                q = frecv[c, 0, slot, :, at]
                g = frecv[c, 1, slot, :, at]
                k = kv_x[c, 0, slot, :, at]
                v = kv_x[c, 1, slot, :, at]
                scores = jnp.where(valid, matmul(q, k, NT) * scaling, -jnp.inf)
                weights = jnp.exp(scores - jnp.max(scores, axis=1, keepdims=True))
                probs = weights / jnp.sum(weights, axis=1, keepdims=True)
                low = probs.astype(BF16)
                dprobs = matmul(g, v, NT)
                delta = jnp.sum(probs * dprobs, axis=1, keepdims=True)
                dscores = (probs * (dprobs - delta)).astype(BF16)
                osend[c, 0, slot, :, at] = matmul(low, v, NN).astype(BF16)
                osend[c, 1, slot, :, at] = (matmul(dscores, k, NN) * scaling).astype(BF16)
                d_x[0, slot, :, at] = (matmul(dscores, q, TN) * scaling).astype(BF16)
                d_x[1, slot, :, at] = matmul(low, g, TN).astype(BF16)
            back_copy(c, slot).start()

    def collect(c):
        @pl.loop(0, enc_count // 256)
        def _(b):
            at = pl.ds(pl.multiple_of(b * 256, 256), 256)
            for a in range(2):
                block = d_x[a].reshape(PARTNERS * ENC_MAX, piece)
                mem_v[a, at, c * piece : (c + 1) * piece] = matmul(
                    grad_m[at, :], block, NN
                ).astype(BF16)

        grad_copy(c).start()

    def finish(c):
        @pl.loop(0, PARTNERS)
        def _(i):
            back_arrival(c, i).wait_recv()

        for a in range(2):
            block = oret[c, a].reshape(PARTNERS * DEC_MAX, piece)
            fin_v[c, a] = matmul(unpack_m[...], block, NN).astype(BF16)
            for step in list(range(1, tensors)) + [0]:
                last_copy(c, a, step).start()

    pack(0)

    for slot in range(PARTNERS):
        shape = (ENC_MAX, enc_count)
        within = iota(shape, 0)
        hits = (iota(shape, 1) - within == meta[2, slot]) & (within < meta[3, slot])
        enc_m[slot // 2, (slot % 2) * ENC_MAX : (slot % 2 + 1) * ENC_MAX, :] = one_hot(hits)
    mem_copy.wait()
    expand(0)
    pack(1)

    position = iota((dec_count, 1), 0)
    goal = jnp.full((dec_count, 1), -1, jnp.int32)
    for i in range(PARTNERS):
        within = position - meta[0, i]
        goal = jnp.where((within >= 0) & (within < meta[1, i]), within + i * DEC_MAX, goal)
    unpack_m[...] = one_hot(iota((dec_count, PARTNERS * DEC_MAX), 1) == goal)
    for b in range(enc_count // 256):
        position = iota((256, 1), 0) + b * 256
        goal = jnp.full((256, 1), -1, jnp.int32)
        for slot in range(PARTNERS):
            within = position - meta[2, slot]
            goal = jnp.where(
                (within >= 0) & (within < meta[3, slot]), within + slot * ENC_MAX, goal
            )
        hits = iota((256, PARTNERS * ENC_MAX), 1) == goal
        grad_m[b * 256 : (b + 1) * 256, :] = one_hot(hits)

    expand(1)
    for c in range(2, CHUNKS):
        pack(c)
        expand(c)
    for c in range(CHUNKS):
        attend(c)
        collect(c)
        if c:
            finish(c - 1)
    finish(CHUNKS - 1)

    for c in range(CHUNKS):
        for a in range(2):
            for step in range(1, tensors):
                first_copy(c, a, step).wait_send()
                last_copy(c, a, step).wait()
            last_copy(c, a, 0).wait()
        grad_copy(c).wait()

        @pl.loop(0, PARTNERS)
        def _(slot):
            forward_copy(c, slot).wait_send()
            back_copy(c, slot).wait_send()


def body(sections, tensors, memory, queries, out_grad, enc_lengths, dec_lengths, readers):
    enc_count, width = memory.shape[1:]
    rows = queries.shape[0]
    dec_count = rows * tensors
    piece = width // CHUNKS
    blocks = (CHUNKS, 2, PARTNERS, DEC_MAX, piece)
    peers = max(tensors - 1, 1)
    anywhere = pl.BlockSpec(memory_space=pl.ANY)
    scalars = pl.BlockSpec(memory_space=pltpu.SMEM)
    dma = pltpu.SemaphoreType.DMA
    return pl.pallas_call(
        functools.partial(kernel, sections, tensors),
        out_shape=(
            jax.ShapeDtypeStruct(queries.shape, BF16),
            jax.ShapeDtypeStruct(queries.shape, BF16),
            jax.ShapeDtypeStruct(memory.shape, BF16),
        ),
        in_specs=[anywhere] * 3 + [scalars] * 3,
        out_specs=(anywhere,) * 3,
        scratch_shapes=[
            pltpu.VMEM((2, enc_count, width), BF16),
            pltpu.VMEM((CHUNKS, 2, dec_count, piece), BF16),
            pltpu.VMEM(blocks, BF16),
            pltpu.VMEM(blocks, BF16),
            pltpu.VMEM(blocks, BF16),
            pltpu.VMEM(blocks, BF16),
            pltpu.VMEM((CHUNKS, 2, dec_count, piece), BF16),
            pltpu.VMEM((CHUNKS, 2, PARTNERS, ENC_MAX, piece), BF16),
            pltpu.VMEM((2, PARTNERS, ENC_MAX, piece), BF16),
            pltpu.VMEM((2, PARTNERS // 2 * DEC_MAX, dec_count), BF16),
            pltpu.VMEM((dec_count, PARTNERS * DEC_MAX), BF16),
            pltpu.VMEM((PARTNERS // 2, 2 * ENC_MAX, enc_count), BF16),
            pltpu.VMEM((enc_count, PARTNERS * ENC_MAX), BF16),
            pltpu.SMEM((4, PARTNERS), jnp.int32),
            dma((CHUNKS, 2, peers)),
            dma((CHUNKS, 2, peers)),
            dma((CHUNKS, 2)),
            dma((CHUNKS, PARTNERS)),
            dma((CHUNKS, PARTNERS)),
            dma((CHUNKS, PARTNERS)),
            dma((CHUNKS, PARTNERS)),
            dma((CHUNKS, 2, peers)),
            dma((CHUNKS, 2, peers)),
            dma((CHUNKS, 2)),
            dma,
            dma((CHUNKS,)),
        ],
        compiler_params=pltpu.CompilerParams(
            collective_id=0, has_side_effects=True, vmem_limit_bytes=60 * 1024 * 1024
        ),
    )(memory, queries, out_grad, enc_lengths, dec_lengths, readers)


def solution(mesh):
    placed = (
        P(None, "section", "tensor"),
        P(("section", "tensor"), None),
        P(("section", "tensor"), None),
        P(),
        P(),
        P(),
    )
    return jax.shard_map(
        functools.partial(body, mesh.shape["section"], mesh.shape["tensor"]),
        mesh=mesh,
        in_specs=placed,
        out_specs=(
            P(("section", "tensor"), None),
            P(("section", "tensor"), None),
            P(None, "section", "tensor"),
        ),
        check_vma=False,
    )
```

```python
import functools

import jax
import jax.numpy as jnp
from jax import lax
from jax.experimental import pallas as pl
from jax.experimental.pallas import tpu as pltpu
from jax.sharding import PartitionSpec as P

HD = 128
ENC_MAX = 128
DEC_MAX = 64
PARTNERS = 8
MOST_CHUNKS = 8
BF16 = jnp.bfloat16
F32 = jnp.float32
MESH = pl.DeviceIdType.MESH


def matmul(a, b, dims):
    return lax.dot_general(a, b, (dims, ((), ())), preferred_element_type=F32)


NN = ((1,), (0,))
NT = ((1,), (1,))
TN = ((0,), (0,))


def chunk_count(width):
    return min(MOST_CHUNKS, width // HD)


def kernel(
    sections,
    tensors,
    mem_hbm,
    q_hbm,
    g_hbm,
    enc_hbm,
    dec_hbm,
    readers_hbm,
    att_out,
    qg_out,
    mg_out,
    mem_v,
    dec_v,
    fsend,
    frecv,
    osend,
    oret,
    fin_v,
    kv_x,
    d_x,
    pack_m,
    unpack_m,
    enc_m,
    grad_m,
    enc_len,
    dec_len,
    readers,
    meta,
    a_send,
    a_recv,
    a_local,
    f_send,
    f_recv,
    o_send,
    o_recv,
    g_send,
    g_recv,
    g_local,
    m_in,
    s_in,
):
    me = lax.axis_index("section")
    mine = lax.axis_index("tensor")
    rows = q_hbm.shape[0]
    enc_count = mem_v.shape[1]
    dec_count = dec_v.shape[2]
    width = mem_v.shape[2]
    chunks = chunk_count(width)
    piece = width // chunks
    spacing = sections // PARTNERS
    scaling = HD ** (-0.5)

    def holder_of(slot):
        return lax.rem(me + 2 * sections - slot * spacing - 1, sections)

    def reader_of(slot):
        return lax.rem(me + slot * spacing + 1, sections)

    half = PARTNERS // 2

    def rank_at(turn):
        other = lax.rem(lax.div(turn, half) + 1 + lax.div(2 * me, sections), 2)
        return other * half + lax.rem(turn + lax.div(me, spacing), half)

    def holder_slot(turn):
        holder = lax.rem(me + sections - 1, spacing) + spacing * rank_at(turn)
        return lax.div(lax.rem(me + sections - holder - 1 + sections, sections), spacing)

    def reader_slot(turn):
        reader = lax.rem(me + 1, spacing) + spacing * rank_at(turn)
        return lax.div(lax.rem(reader + 2 * sections - me - 1, sections), spacing)

    def peer_of(step):
        return lax.rem(mine + step, tensors)

    mem_copy = pltpu.make_async_copy(mem_hbm, mem_v, m_in)
    scalar_copies = [
        pltpu.make_async_copy(source, target, s_in.at[i])
        for i, (source, target) in enumerate(
            ((enc_hbm, enc_len), (dec_hbm, dec_len), (readers_hbm, readers))
        )
    ]
    for copy in scalar_copies:
        copy.start()

    barrier = pltpu.get_barrier_semaphore()
    for step in range(1, tensors):
        pl.semaphore_signal(
            barrier, inc=1, device_id={"tensor": peer_of(step)}, device_id_type=MESH
        )
    for slot in range(PARTNERS):
        pl.semaphore_signal(
            barrier, inc=1, device_id={"section": holder_of(slot)}, device_id_type=MESH
        )
        pl.semaphore_signal(
            barrier, inc=1, device_id={"section": reader_of(slot)}, device_id_type=MESH
        )
    pl.semaphore_wait(barrier, tensors - 1 + 2 * PARTNERS)

    own_rows = pl.ds(pl.multiple_of(mine * rows, rows), rows)

    def first_copy(c, a, step):
        peer = peer_of(step)
        source = (q_hbm, g_hbm)[a]
        columns = pl.ds(pl.multiple_of(peer * width + c * piece, piece), piece)
        if step == 0:
            return pltpu.make_async_copy(
                source.at[:, columns], dec_v.at[c, a, own_rows], a_local.at[c, a]
            )
        return pltpu.make_async_remote_copy(
            src_ref=source.at[:, columns],
            dst_ref=dec_v.at[c, a, own_rows],
            send_sem=a_send.at[c, a, step - 1],
            recv_sem=a_recv.at[c, a, step - 1],
            device_id={"tensor": peer},
            device_id_type=MESH,
        )

    def fetch(c):
        for a in range(2):
            for step in list(range(1, tensors)) + [0]:
                first_copy(c, a, step).start()

    fetch(0)
    mem_copy.start()
    for copy in scalar_copies:
        copy.wait()

    start = jnp.int32(0)
    for i in range(PARTNERS):
        length = dec_len[i, me]
        meta[0, i] = start
        meta[1, i] = length
        start = start + length
    for slot in range(PARTNERS):
        reader = reader_of(slot)
        start, begin, size = jnp.int32(0), jnp.int32(0), jnp.int32(0)
        for j in range(PARTNERS):
            length = enc_len[j, me]
            match = readers[j, me] == reader
            begin = jnp.where(match, start, begin)
            size = jnp.where(match, length, size)
            start = start + length
        meta[2, slot] = begin
        meta[3, slot] = size

    def one_hot(hits):
        return jnp.where(hits, 1.0, 0.0).astype(BF16)

    def iota(shape, dim):
        return lax.broadcasted_iota(jnp.int32, shape, dim)

    for i in range(PARTNERS):
        shape = (DEC_MAX, dec_count)
        within = iota(shape, 0)
        hits = (iota(shape, 1) - within == meta[0, i]) & (within < meta[1, i])
        pack_m[i // half, (i % half) * DEC_MAX : (i % half + 1) * DEC_MAX, :] = one_hot(hits)

    def forward_copy(c, slot):
        holder = holder_of(slot)
        return pltpu.make_async_remote_copy(
            src_ref=fsend.at[c, :, lax.div(holder, spacing)],
            dst_ref=frecv.at[c, :, slot],
            send_sem=f_send.at[c, slot],
            recv_sem=f_recv.at[c, slot],
            device_id={"section": holder},
            device_id_type=MESH,
        )

    def back_copy(c, slot):
        return pltpu.make_async_remote_copy(
            src_ref=osend.at[c, :, slot],
            dst_ref=oret.at[c, :, lax.div(me, spacing)],
            send_sem=o_send.at[c, slot],
            recv_sem=o_recv.at[c, lax.div(me, spacing)],
            device_id={"section": reader_of(slot)},
            device_id_type=MESH,
        )

    def back_arrival(c, i):
        return pltpu.make_async_remote_copy(
            src_ref=osend.at[c, :, i],
            dst_ref=oret.at[c, :, i],
            send_sem=o_send.at[c, i],
            recv_sem=o_recv.at[c, i],
            device_id={"section": reader_of(i)},
            device_id_type=MESH,
        )

    def last_copy(c, a, step):
        peer = peer_of(step)
        target = (att_out, qg_out)[a]
        source = fin_v.at[c, a, pl.ds(pl.multiple_of(peer * rows, rows), rows)]
        columns = pl.ds(pl.multiple_of(mine * width + c * piece, piece), piece)
        if step == 0:
            return pltpu.make_async_copy(source, target.at[:, columns], g_local.at[c, a])
        return pltpu.make_async_remote_copy(
            src_ref=source,
            dst_ref=target.at[:, columns],
            send_sem=g_send.at[c, a, step - 1],
            recv_sem=g_recv.at[c, a, step - 1],
            device_id={"tensor": peer},
            device_id_type=MESH,
        )

    def pack(c):
        for a in range(2):
            first_copy(c, a, 0).wait()
            for step in range(1, tensors):
                first_copy(c, a, step).wait_recv()
        if c + 1 < chunks:
            fetch(c + 1)
        for a in range(2):
            for g in range(2):
                block = matmul(pack_m[g], dec_v[c, a], NN).astype(BF16)
                fsend[c, a, g * half : (g + 1) * half] = block.reshape(half, DEC_MAX, piece)

        @pl.loop(0, PARTNERS)
        def _(turn):
            forward_copy(c, holder_slot(jnp.int32(turn))).start()

    def expand(c):
        @pl.loop(0, PARTNERS // 2)
        def _(g):
            for a in range(2):
                block = matmul(enc_m[g], mem_v[a, :, c * piece : (c + 1) * piece], NN)
                kv_x[c, a, pl.ds(g * 2, 2)] = block.astype(BF16).reshape(2, ENC_MAX, piece)

    def attend(c):
        @pl.loop(0, PARTNERS)
        def _(turn):
            slot = reader_slot(jnp.int32(turn))
            forward_copy(c, slot).wait_recv()
            valid = iota((DEC_MAX, ENC_MAX), 1) < meta[3, slot]
            for h in range(piece // HD):
                at = slice(h * HD, (h + 1) * HD)
                q = frecv[c, 0, slot, :, at]
                g = frecv[c, 1, slot, :, at]
                k = kv_x[c, 0, slot, :, at]
                v = kv_x[c, 1, slot, :, at]
                scores = jnp.where(valid, matmul(q, k, NT) * scaling, -jnp.inf)
                weights = jnp.exp(scores - jnp.max(scores, axis=1, keepdims=True))
                probs = weights / jnp.sum(weights, axis=1, keepdims=True)
                low = probs.astype(BF16)
                dprobs = matmul(g, v, NT)
                delta = jnp.sum(probs * dprobs, axis=1, keepdims=True)
                dscores = (probs * (dprobs - delta)).astype(BF16)
                osend[c, 0, slot, :, at] = matmul(low, v, NN).astype(BF16)
                osend[c, 1, slot, :, at] = (matmul(dscores, k, NN) * scaling).astype(BF16)
                d_x[0, slot, :, at] = (matmul(dscores, q, TN) * scaling).astype(BF16)
                d_x[1, slot, :, at] = matmul(low, g, TN).astype(BF16)
            back_copy(c, slot).start()

    def collect(c):
        @pl.loop(0, enc_count // 256)
        def _(b):
            at = pl.ds(pl.multiple_of(b * 256, 256), 256)
            for a in range(2):
                block = d_x[a].reshape(PARTNERS * ENC_MAX, piece)
                mg_out[a, at, c * piece : (c + 1) * piece] = matmul(
                    grad_m[at, :], block, NN
                ).astype(BF16)

    def finish(c):
        @pl.loop(0, PARTNERS)
        def _(i):
            back_arrival(c, i).wait_recv()

        for a in range(2):
            block = oret[c, a].reshape(PARTNERS * DEC_MAX, piece)
            fin_v[c, a] = matmul(unpack_m[...], block, NN).astype(BF16)
            for step in list(range(1, tensors)) + [0]:
                last_copy(c, a, step).start()

    pack(0)

    for slot in range(PARTNERS):
        shape = (ENC_MAX, enc_count)
        within = iota(shape, 0)
        hits = (iota(shape, 1) - within == meta[2, slot]) & (within < meta[3, slot])
        enc_m[slot // 2, (slot % 2) * ENC_MAX : (slot % 2 + 1) * ENC_MAX, :] = one_hot(hits)
    mem_copy.wait()
    expand(0)
    pack(1)

    position = iota((dec_count, 1), 0)
    goal = jnp.full((dec_count, 1), -1, jnp.int32)
    for i in range(PARTNERS):
        within = position - meta[0, i]
        goal = jnp.where((within >= 0) & (within < meta[1, i]), within + i * DEC_MAX, goal)
    unpack_m[...] = one_hot(iota((dec_count, PARTNERS * DEC_MAX), 1) == goal)
    for b in range(enc_count // 256):
        position = iota((256, 1), 0) + b * 256
        goal = jnp.full((256, 1), -1, jnp.int32)
        for slot in range(PARTNERS):
            within = position - meta[2, slot]
            goal = jnp.where(
                (within >= 0) & (within < meta[3, slot]), within + slot * ENC_MAX, goal
            )
        hits = iota((256, PARTNERS * ENC_MAX), 1) == goal
        grad_m[b * 256 : (b + 1) * 256, :] = one_hot(hits)

    expand(1)
    for c in range(2, chunks):
        pack(c)
        expand(c)
    for c in range(chunks):
        attend(c)
        collect(c)
        if c:
            finish(c - 1)
    finish(chunks - 1)

    for c in range(chunks):
        for a in range(2):
            for step in range(1, tensors):
                first_copy(c, a, step).wait_send()
                last_copy(c, a, step).wait()
            last_copy(c, a, 0).wait()

        @pl.loop(0, PARTNERS)
        def _(slot):
            forward_copy(c, slot).wait_send()
            back_copy(c, slot).wait_send()


def body(sections, tensors, memory, queries, out_grad, enc_lengths, dec_lengths, readers):
    enc_count, width = memory.shape[1:]
    rows = queries.shape[0]
    dec_count = rows * tensors
    chunks = chunk_count(width)
    piece = width // chunks
    blocks = (chunks, 2, PARTNERS, DEC_MAX, piece)
    peers = max(tensors - 1, 1)
    scalars = (enc_lengths.T, dec_lengths.T, readers.T)
    anywhere = pl.BlockSpec(memory_space=pl.ANY)
    resident = pl.BlockSpec(memory_space=pltpu.VMEM)
    dma = pltpu.SemaphoreType.DMA
    return pl.pallas_call(
        functools.partial(kernel, sections, tensors),
        out_shape=(
            pltpu.VMEM(queries.shape, BF16),
            pltpu.VMEM(queries.shape, BF16),
            pltpu.VMEM(memory.shape, BF16),
        ),
        in_specs=[anywhere] * 6,
        out_specs=(resident,) * 3,
        scratch_shapes=[
            pltpu.VMEM((2, enc_count, width), BF16),
            pltpu.VMEM((chunks, 2, dec_count, piece), BF16),
            pltpu.VMEM(blocks, BF16),
            pltpu.VMEM(blocks, BF16),
            pltpu.VMEM(blocks, BF16),
            pltpu.VMEM(blocks, BF16),
            pltpu.VMEM((chunks, 2, dec_count, piece), BF16),
            pltpu.VMEM((chunks, 2, PARTNERS, ENC_MAX, piece), BF16),
            pltpu.VMEM((2, PARTNERS, ENC_MAX, piece), BF16),
            pltpu.VMEM((2, PARTNERS // 2 * DEC_MAX, dec_count), BF16),
            pltpu.VMEM((dec_count, PARTNERS * DEC_MAX), BF16),
            pltpu.VMEM((PARTNERS // 2, 2 * ENC_MAX, enc_count), BF16),
            pltpu.VMEM((enc_count, PARTNERS * ENC_MAX), BF16),
            *[pltpu.SMEM(array.shape, jnp.int32) for array in scalars],
            pltpu.SMEM((4, PARTNERS), jnp.int32),
            dma((chunks, 2, peers)),
            dma((chunks, 2, peers)),
            dma((chunks, 2)),
            dma((chunks, PARTNERS)),
            dma((chunks, PARTNERS)),
            dma((chunks, PARTNERS)),
            dma((chunks, PARTNERS)),
            dma((chunks, 2, peers)),
            dma((chunks, 2, peers)),
            dma((chunks, 2)),
            dma,
            dma((3,)),
        ],
        compiler_params=pltpu.CompilerParams(
            collective_id=0, has_side_effects=True, vmem_limit_bytes=46 * 1024 * 1024
        ),
    )(memory, queries, out_grad, *scalars)


def solution(mesh):
    placed = (
        P(None, "section", "tensor"),
        P(("section", "tensor"), None),
        P(("section", "tensor"), None),
        P(),
        P(),
        P(),
    )
    return jax.shard_map(
        functools.partial(body, mesh.shape["section"], mesh.shape["tensor"]),
        mesh=mesh,
        in_specs=placed,
        out_specs=(
            P(("section", "tensor"), None),
            P(("section", "tensor"), None),
            P(None, "section", "tensor"),
        ),
        check_vma=False,
    )
```

```python
import functools

import jax
import jax.numpy as jnp
from jax import lax
from jax.experimental import pallas as pl
from jax.experimental.pallas import tpu as pltpu
from jax.sharding import PartitionSpec as P

HD = 128
ENC_MAX = 128
DEC_MAX = 64
PARTNERS = 8
MOST_CHUNKS = 8
BF16 = jnp.bfloat16
F32 = jnp.float32
MESH = pl.DeviceIdType.MESH


def matmul(a, b, dims):
    return lax.dot_general(a, b, (dims, ((), ())), preferred_element_type=F32)


NN = ((1,), (0,))
NT = ((1,), (1,))
TN = ((0,), (0,))


def chunk_count(width):
    return min(MOST_CHUNKS, width // HD)


def kernel(
    sections,
    tensors,
    mem_hbm,
    q_hbm,
    g_hbm,
    enc_hbm,
    dec_hbm,
    readers_hbm,
    att_out,
    qg_out,
    mg_out,
    mem_v,
    dec_v,
    fsend,
    frecv,
    osend,
    oret,
    fin_v,
    kv_x,
    d_x,
    pack_m,
    unpack_m,
    enc_m,
    grad_m,
    enc_len,
    dec_len,
    readers,
    meta,
    a_send,
    a_recv,
    a_local,
    f_send,
    f_recv,
    o_send,
    o_recv,
    g_send,
    g_recv,
    g_local,
    m_in,
    s_in,
):
    me = lax.axis_index("section")
    mine = lax.axis_index("tensor")
    rows = q_hbm.shape[0]
    enc_count = mem_v.shape[1]
    dec_count = dec_v.shape[2]
    width = mem_v.shape[2]
    chunks = chunk_count(width)
    piece = width // chunks
    spacing = sections // PARTNERS
    scaling = HD ** (-0.5)

    def holder_of(slot):
        return lax.rem(me + 2 * sections - slot * spacing - 1, sections)

    def reader_of(slot):
        return lax.rem(me + slot * spacing + 1, sections)

    half = PARTNERS // 2

    def peer_of(step):
        return lax.rem(mine + step, tensors)

    mem_copy = pltpu.make_async_copy(mem_hbm, mem_v, m_in)
    scalar_copies = [
        pltpu.make_async_copy(source, target, s_in.at[i])
        for i, (source, target) in enumerate(
            ((enc_hbm, enc_len), (dec_hbm, dec_len), (readers_hbm, readers))
        )
    ]
    for copy in scalar_copies:
        copy.start()

    barrier = pltpu.get_barrier_semaphore()
    for step in range(1, tensors):
        pl.semaphore_signal(
            barrier, inc=1, device_id={"tensor": peer_of(step)}, device_id_type=MESH
        )
    for slot in range(PARTNERS):
        pl.semaphore_signal(
            barrier, inc=1, device_id={"section": holder_of(slot)}, device_id_type=MESH
        )
        pl.semaphore_signal(
            barrier, inc=1, device_id={"section": reader_of(slot)}, device_id_type=MESH
        )
    pl.semaphore_wait(barrier, tensors - 1 + 2 * PARTNERS)

    own_rows = pl.ds(pl.multiple_of(mine * rows, rows), rows)

    def first_copy(c, a, step):
        peer = peer_of(step)
        source = (q_hbm, g_hbm)[a]
        columns = pl.ds(pl.multiple_of(peer * width + c * piece, piece), piece)
        if step == 0:
            return pltpu.make_async_copy(
                source.at[:, columns], dec_v.at[c, a, own_rows], a_local.at[c, a]
            )
        return pltpu.make_async_remote_copy(
            src_ref=source.at[:, columns],
            dst_ref=dec_v.at[c, a, own_rows],
            send_sem=a_send.at[c, a, step - 1],
            recv_sem=a_recv.at[c, a, step - 1],
            device_id={"tensor": peer},
            device_id_type=MESH,
        )

    def fetch(c):
        for a in range(2):
            for step in list(range(1, tensors)) + [0]:
                first_copy(c, a, step).start()

    fetch(0)
    mem_copy.start()
    for copy in scalar_copies:
        copy.wait()

    start = jnp.int32(0)
    for i in range(PARTNERS):
        length = dec_len[i, me]
        meta[0, i] = start
        meta[1, i] = length
        start = start + length
    for slot in range(PARTNERS):
        reader = reader_of(slot)
        start, begin, size = jnp.int32(0), jnp.int32(0), jnp.int32(0)
        for j in range(PARTNERS):
            length = enc_len[j, me]
            match = readers[j, me] == reader
            begin = jnp.where(match, start, begin)
            size = jnp.where(match, length, size)
            start = start + length
        meta[2, slot] = begin
        meta[3, slot] = size

    def one_hot(hits):
        return jnp.where(hits, 1.0, 0.0).astype(BF16)

    def iota(shape, dim):
        return lax.broadcasted_iota(jnp.int32, shape, dim)

    for i in range(PARTNERS):
        shape = (DEC_MAX, dec_count)
        within = iota(shape, 0)
        hits = (iota(shape, 1) - within == meta[0, i]) & (within < meta[1, i])
        pack_m[i // half, (i % half) * DEC_MAX : (i % half + 1) * DEC_MAX, :] = one_hot(hits)

    def forward_copy(c, slot):
        holder = holder_of(slot)
        return pltpu.make_async_remote_copy(
            src_ref=fsend.at[c, :, lax.div(holder, spacing)],
            dst_ref=frecv.at[c, :, slot],
            send_sem=f_send.at[c, slot],
            recv_sem=f_recv.at[c, slot],
            device_id={"section": holder},
            device_id_type=MESH,
        )

    def back_copy(c, slot):
        return pltpu.make_async_remote_copy(
            src_ref=osend.at[c, :, slot],
            dst_ref=oret.at[c, :, lax.div(me, spacing)],
            send_sem=o_send.at[c, slot],
            recv_sem=o_recv.at[c, lax.div(me, spacing)],
            device_id={"section": reader_of(slot)},
            device_id_type=MESH,
        )

    def back_arrival(c, i):
        return pltpu.make_async_remote_copy(
            src_ref=osend.at[c, :, i],
            dst_ref=oret.at[c, :, i],
            send_sem=o_send.at[c, i],
            recv_sem=o_recv.at[c, i],
            device_id={"section": reader_of(i)},
            device_id_type=MESH,
        )

    def last_copy(c, a, step):
        peer = peer_of(step)
        target = (att_out, qg_out)[a]
        source = fin_v.at[c, a, pl.ds(pl.multiple_of(peer * rows, rows), rows)]
        columns = pl.ds(pl.multiple_of(mine * width + c * piece, piece), piece)
        if step == 0:
            return pltpu.make_async_copy(source, target.at[:, columns], g_local.at[c, a])
        return pltpu.make_async_remote_copy(
            src_ref=source,
            dst_ref=target.at[:, columns],
            send_sem=g_send.at[c, a, step - 1],
            recv_sem=g_recv.at[c, a, step - 1],
            device_id={"tensor": peer},
            device_id_type=MESH,
        )

    def pack(c):
        for a in range(2):
            first_copy(c, a, 0).wait()
            for step in range(1, tensors):
                first_copy(c, a, step).wait_recv()
        if c + 1 < chunks:
            fetch(c + 1)
        for a in range(2):
            for g in range(2):
                block = matmul(pack_m[g], dec_v[c, a], NN).astype(BF16)
                fsend[c, a, g * half : (g + 1) * half] = block.reshape(half, DEC_MAX, piece)

        @pl.loop(0, PARTNERS)
        def _(turn):
            forward_copy(c, turn).start()

    def expand(c):
        @pl.loop(0, PARTNERS // 2)
        def _(g):
            for a in range(2):
                block = matmul(enc_m[g], mem_v[a, :, c * piece : (c + 1) * piece], NN)
                kv_x[c, a, pl.ds(g * 2, 2)] = block.astype(BF16).reshape(2, ENC_MAX, piece)

    def attend(c):
        @pl.loop(0, PARTNERS)
        def _(turn):
            slot = turn
            forward_copy(c, slot).wait_recv()
            valid = iota((DEC_MAX, ENC_MAX), 1) < meta[3, slot]
            for h in range(piece // HD):
                at = slice(h * HD, (h + 1) * HD)
                q = frecv[c, 0, slot, :, at]
                g = frecv[c, 1, slot, :, at]
                k = kv_x[c, 0, slot, :, at]
                v = kv_x[c, 1, slot, :, at]
                scores = jnp.where(valid, matmul(q, k, NT) * scaling, -jnp.inf)
                weights = jnp.exp(scores - jnp.max(scores, axis=1, keepdims=True))
                probs = weights / jnp.sum(weights, axis=1, keepdims=True)
                low = probs.astype(BF16)
                dprobs = matmul(g, v, NT)
                delta = jnp.sum(probs * dprobs, axis=1, keepdims=True)
                dscores = (probs * (dprobs - delta)).astype(BF16)
                osend[c, 0, slot, :, at] = matmul(low, v, NN).astype(BF16)
                osend[c, 1, slot, :, at] = (matmul(dscores, k, NN) * scaling).astype(BF16)
                d_x[0, slot, :, at] = (matmul(dscores, q, TN) * scaling).astype(BF16)
                d_x[1, slot, :, at] = matmul(low, g, TN).astype(BF16)
            back_copy(c, slot).start()

    def collect(c):
        @pl.loop(0, enc_count // 256)
        def _(b):
            at = pl.ds(pl.multiple_of(b * 256, 256), 256)
            for a in range(2):
                block = d_x[a].reshape(PARTNERS * ENC_MAX, piece)
                mg_out[a, at, c * piece : (c + 1) * piece] = matmul(
                    grad_m[at, :], block, NN
                ).astype(BF16)

    def finish(c):
        @pl.loop(0, PARTNERS)
        def _(i):
            back_arrival(c, i).wait_recv()

        for a in range(2):
            block = oret[c, a].reshape(PARTNERS * DEC_MAX, piece)
            fin_v[c, a] = matmul(unpack_m[...], block, NN).astype(BF16)
            for step in list(range(1, tensors)) + [0]:
                last_copy(c, a, step).start()

    def settle():
        for c in range(chunks):
            for a in range(2):
                for step in range(1, tensors):
                    first_copy(c, a, step).wait_send()

            @pl.loop(0, PARTNERS)
            def _(slot):
                forward_copy(c, slot).wait_send()
                back_copy(c, slot).wait_send()

    pack(0)

    for slot in range(PARTNERS):
        shape = (ENC_MAX, enc_count)
        within = iota(shape, 0)
        hits = (iota(shape, 1) - within == meta[2, slot]) & (within < meta[3, slot])
        enc_m[slot // 2, (slot % 2) * ENC_MAX : (slot % 2 + 1) * ENC_MAX, :] = one_hot(hits)
    mem_copy.wait()
    expand(0)
    pack(1)

    position = iota((dec_count, 1), 0)
    goal = jnp.full((dec_count, 1), -1, jnp.int32)
    for i in range(PARTNERS):
        within = position - meta[0, i]
        goal = jnp.where((within >= 0) & (within < meta[1, i]), within + i * DEC_MAX, goal)
    unpack_m[...] = one_hot(iota((dec_count, PARTNERS * DEC_MAX), 1) == goal)
    for b in range(enc_count // 256):
        position = iota((256, 1), 0) + b * 256
        goal = jnp.full((256, 1), -1, jnp.int32)
        for slot in range(PARTNERS):
            within = position - meta[2, slot]
            goal = jnp.where(
                (within >= 0) & (within < meta[3, slot]), within + slot * ENC_MAX, goal
            )
        hits = iota((256, PARTNERS * ENC_MAX), 1) == goal
        grad_m[b * 256 : (b + 1) * 256, :] = one_hot(hits)

    expand(1)
    for c in range(2, chunks):
        pack(c)
        expand(c)
    for c in range(chunks):
        attend(c)
        collect(c)
        if c >= 3:
            finish(c - 3)
    for c in range(max(chunks - 3, 0), chunks):
        if c == chunks - 1:
            settle()
        finish(c)

    for c in range(chunks):
        for a in range(2):
            for step in range(1, tensors):
                last_copy(c, a, step).wait()
            last_copy(c, a, 0).wait()


def body(sections, tensors, memory, queries, out_grad, enc_lengths, dec_lengths, readers):
    enc_count, width = memory.shape[1:]
    rows = queries.shape[0]
    dec_count = rows * tensors
    chunks = chunk_count(width)
    piece = width // chunks
    blocks = (chunks, 2, PARTNERS, DEC_MAX, piece)
    peers = max(tensors - 1, 1)
    scalars = (enc_lengths.T, dec_lengths.T, readers.T)
    anywhere = pl.BlockSpec(memory_space=pl.ANY)
    resident = pl.BlockSpec(memory_space=pltpu.VMEM)
    dma = pltpu.SemaphoreType.DMA
    return pl.pallas_call(
        functools.partial(kernel, sections, tensors),
        out_shape=(
            pltpu.VMEM(queries.shape, BF16),
            pltpu.VMEM(queries.shape, BF16),
            pltpu.VMEM(memory.shape, BF16),
        ),
        in_specs=[anywhere] * 6,
        out_specs=(resident,) * 3,
        scratch_shapes=[
            pltpu.VMEM((2, enc_count, width), BF16),
            pltpu.VMEM((chunks, 2, dec_count, piece), BF16),
            pltpu.VMEM(blocks, BF16),
            pltpu.VMEM(blocks, BF16),
            pltpu.VMEM(blocks, BF16),
            pltpu.VMEM(blocks, BF16),
            pltpu.VMEM((chunks, 2, dec_count, piece), BF16),
            pltpu.VMEM((chunks, 2, PARTNERS, ENC_MAX, piece), BF16),
            pltpu.VMEM((2, PARTNERS, ENC_MAX, piece), BF16),
            pltpu.VMEM((2, PARTNERS // 2 * DEC_MAX, dec_count), BF16),
            pltpu.VMEM((dec_count, PARTNERS * DEC_MAX), BF16),
            pltpu.VMEM((PARTNERS // 2, 2 * ENC_MAX, enc_count), BF16),
            pltpu.VMEM((enc_count, PARTNERS * ENC_MAX), BF16),
            *[pltpu.SMEM(array.shape, jnp.int32) for array in scalars],
            pltpu.SMEM((4, PARTNERS), jnp.int32),
            dma((chunks, 2, peers)),
            dma((chunks, 2, peers)),
            dma((chunks, 2)),
            dma((chunks, PARTNERS)),
            dma((chunks, PARTNERS)),
            dma((chunks, PARTNERS)),
            dma((chunks, PARTNERS)),
            dma((chunks, 2, peers)),
            dma((chunks, 2, peers)),
            dma((chunks, 2)),
            dma,
            dma((3,)),
        ],
        compiler_params=pltpu.CompilerParams(
            collective_id=0, has_side_effects=True, vmem_limit_bytes=46 * 1024 * 1024
        ),
    )(memory, queries, out_grad, *scalars)


def solution(mesh):
    placed = (
        P(None, "section", "tensor"),
        P(("section", "tensor"), None),
        P(("section", "tensor"), None),
        P(),
        P(),
        P(),
    )
    return jax.shard_map(
        functools.partial(body, mesh.shape["section"], mesh.shape["tensor"]),
        mesh=mesh,
        in_specs=placed,
        out_specs=(
            P(("section", "tensor"), None),
            P(("section", "tensor"), None),
            P(None, "section", "tensor"),
        ),
        check_vma=False,
    )
```
